128 devices in a mesh: seq: 16 (over y_lo, x, core), head: 8 (over z, y_hi).
Axes of the slice: x: 4, y: 4 (y_hi: 2, y_lo: 2; y = y_hi * 2 + y_lo), z: 4, core: 2. Of those that a mesh axis runs over, the one named last changes fastest.
Arguments:
- queries: bfloat16 [12288, 5120], P(('seq', 'head')), may hold values from -18 to 18
- keys: bfloat16 [12288, 5120], P(('seq', 'head')), may hold values from -18 to 18
- values: bfloat16 [12288, 5120], P(('seq', 'head')), may hold values from -6 to 6
- pairs: int32 [32, 4], P('seq'), may hold values from 0 to 31, as said below
- pair_count: int32 [32], P('seq'), may hold values from 3 to 4, as said below
Outputs:
- attended: bfloat16 [12288, 5120], P(('seq', 'head'))
The draws below stay inside these ranges and needn't reach their ends.
Inputs may be any that keep to these rules, and one draw needn't show every extreme that they name: `pairs`: row g names 4 distinct tiles whose time, height and width coordinates each differ from those of tile g by at most one; its first entry is g itself. `pair_count`: some tile uses all 4 listed tiles.
All inputs are finite; a program needn't handle non-finite values.
Results may differ from the reference program's by a relative error of at most 0.0047.
Values may be sent and summed in bfloat16 or wider, within the bound.
No kernel may reach another device: no remote copies, remote signals or barrier semaphores. Data moves between devices by JAX's collectives and lax.ppermute only.
A program may use at most 256 MiB of HBM per device.

```python
import math
import jax
import jax.numpy as jnp
from jax import lax

HEAD_DIM = 128
D = 5120
TILE = 384
GRID_H = 4
GRID_W = 2
MAXK = 4
TILES_ALL = 32
TOKENS = 12288


def draw_queries(key, part):
    key = jax.random.fold_in(key, 3)
    result = jnp.clip(jax.random.normal(key, (TOKENS, D), jnp.float32), -4.0, 4.0)
    return result.astype(jnp.bfloat16)


def draw_keys(key, part):
    key = jax.random.fold_in(key, 5)
    result = jnp.clip(jax.random.normal(key, (TOKENS, D), jnp.float32), -4.0, 4.0)
    return result.astype(jnp.bfloat16)


def draw_pairs(key, part):
    key = jax.random.fold_in(key, 11)
    per_time = GRID_H * GRID_W
    tile_index = jnp.arange(TILES_ALL, dtype=jnp.int32)
    tile_time = tile_index // per_time
    tile_row = tile_index // GRID_W % GRID_H
    tile_col = tile_index % GRID_W
    offset = jnp.arange(27, dtype=jnp.int32)
    time_step = offset[None, :] // 9
    near_time = tile_time[:, None] + time_step - 1
    near_row = tile_row[:, None] + offset[None, :] // 3 % 3 - 1
    near_col = tile_col[:, None] + offset[None, :] % 3 - 1
    inside = (near_time >= 0) & (near_time < TILES_ALL // per_time)
    inside = inside & (near_row >= 0) & (near_row < GRID_H) & (near_col >= 0) & (near_col < GRID_W)
    base = jax.random.randint(key, (TILES_ALL, 27), 0, 1 << 20, dtype=jnp.int32) * 32 + offset[None, :]
    prev_band = inside & (time_step == 0)
    next_band = inside & (time_step == 2)
    first_prev = jnp.argmin(jnp.where(prev_band, base, 1 << 27), axis=1).astype(jnp.int32)
    first_next = jnp.argmin(jnp.where(next_band, base, 1 << 27), axis=1).astype(jnp.int32)
    has_prev = jnp.any(prev_band, axis=1)
    has_next = jnp.any(next_band, axis=1)
    ranking = base + jnp.where(time_step == 1, 0, 1 << 25)
    ranking = jnp.where(inside, ranking, 1 << 27)
    ranking = jnp.where((offset[None, :] == first_next[:, None]) & has_next[:, None], -1, ranking)
    ranking = jnp.where((offset[None, :] == first_prev[:, None]) & has_prev[:, None], -2, ranking)
    ranking = jnp.where(offset[None, :] == 13, -3, ranking)
    chosen = jnp.argsort(ranking, axis=1)[:, :MAXK]
    target = near_time * per_time + near_row * GRID_W + near_col
    return jnp.take_along_axis(target, chosen, axis=1).astype(jnp.int32)


def draw_pair_count(key, part):
    key = jax.random.fold_in(key, 17)
    counts = jax.random.randint(key, (TILES_ALL,), 3, MAXK + 1, dtype=jnp.int32)
    chosen = jax.random.randint(jax.random.fold_in(key, 1), (), 0, TILES_ALL // 2, dtype=jnp.int32)
    other = chosen + TILES_ALL // 2
    counts = counts.at[chosen].set(MAXK)
    counts = counts.at[other].set(3)
    return counts.astype(jnp.int32)


def block_levels(key, extent, cuts, least, high):
    loudness = 1.0
    for position, blocks in cuts:
        steps = jax.random.uniform(jax.random.fold_in(jax.random.fold_in(key, 6), position), (blocks,), jnp.float32, least / len(cuts), high / len(cuts))
        loudness = loudness * jnp.repeat(jnp.exp(steps), extent[position] // blocks).reshape((-1,) + (1,) * (len(extent) - 1 - position))
    return loudness


def gaussian(key, extent, width, bound, cuts=(), held_as=jnp.bfloat16):
    values = width * jax.random.normal(key, extent, jnp.float32)
    if cuts:
        values = values * block_levels(key, extent, cuts, -0.22, 0.18)
    return jnp.clip(values, -bound, bound).astype(held_as)


def setup_inputs(seed: int = 0) -> dict:
    splits = jax.random.split(jax.random.key(seed), 6)
    return {
        "queries": draw_queries(jax.random.fold_in(splits[5], 71), 0),
        "keys": draw_keys(jax.random.fold_in(splits[5], 71), 0),
        "values": gaussian(splits[2], (TOKENS, D), 1.0, 6.0, ((0, 128),)),
        "pairs": draw_pairs(jax.random.fold_in(splits[5], 71), 0),
        "pair_count": draw_pair_count(jax.random.fold_in(splits[5], 71), 0),
    }


def reference(queries, keys, values, pairs, pair_count):
    token_count, feat_width = queries.shape
    head_count = feat_width // HEAD_DIM
    score_scale = 1.0 / math.sqrt(HEAD_DIM)
    query_tiles = queries.reshape(TILES_ALL, TILE, head_count, HEAD_DIM)
    key_tiles = keys.reshape(TILES_ALL, TILE, head_count, HEAD_DIM)
    value_tiles = values.reshape(TILES_ALL, TILE, head_count, HEAD_DIM)

    def one_tile(packed):
        query_tile, tile_list, live_count = packed
        key_rows = key_tiles[tile_list].reshape(MAXK * TILE, head_count, HEAD_DIM)
        value_rows = value_tiles[tile_list].reshape(MAXK * TILE, head_count, HEAD_DIM)
        live_slot = jnp.repeat(jnp.arange(MAXK) < live_count, TILE)[None, None, :]
        scores = jnp.einsum('qhd,khd->hqk', query_tile.astype(jnp.float32), key_rows.astype(jnp.float32)) * score_scale
        peak = lax.optimization_barrier(jnp.max(jnp.where(live_slot, scores, -jnp.inf), axis=-1, keepdims=True))
        exps = jnp.where(live_slot, jnp.exp(scores - peak), 0.0)
        weight_sum = lax.optimization_barrier(jnp.sum(exps, axis=-1))
        probs = exps.astype(jnp.bfloat16)
        output = jnp.einsum('hqk,khd->qhd', probs.astype(jnp.float32), value_rows.astype(jnp.float32))
        output = output / jnp.transpose(weight_sum)[:, :, None]
        return output.astype(jnp.bfloat16).reshape(TILE, feat_width)
    result = lax.map(one_tile, (query_tiles, pairs, pair_count))
    return result.reshape(token_count, feat_width)
```

```python
import functools
import math

import jax
import jax.numpy as jnp
from jax import lax
from jax.experimental import pallas as pl
from jax.experimental.pallas import tpu as pltpu
from jax.sharding import PartitionSpec as P

HEAD_DIM = 128
MAXK = 4
CORES = 2
MIB = 1 << 20


def pack_kernel(q_ref, k_ref, v_ref, o_ref):
    half = q_ref.shape[0] // CORES
    heads = q_ref.shape[1] // HEAD_DIM
    for core in range(CORES):
        rows = pl.ds(core * half, half)
        for h in range(heads):
            cols = pl.ds(h * HEAD_DIM, HEAD_DIM)
            for part, ref in enumerate((k_ref, v_ref, q_ref)):
                o_ref[core * heads + h, pl.ds(part * half, half), :] = ref[rows, cols]


def unpack_kernel(i_ref, o_ref):
    half = i_ref.shape[1]
    heads = i_ref.shape[0] // CORES
    for core in range(CORES):
        for h in range(heads):
            o_ref[pl.ds(core * half, half), pl.ds(h * HEAD_DIM, HEAD_DIM)] = i_ref[core * heads + h]


def attend_kernel(pairs_ref, own_ref, sib_ref, o_ref, *, sources, half):
    g = pl.program_id(0)
    tile_half = sources * half
    factor = math.log2(math.e) / math.sqrt(HEAD_DIM)

    def rows(ref, tile, part):
        block = ref[pl.ds(tile * sources, sources), pl.ds(part * half, half), :]
        return block.reshape(tile_half, HEAD_DIM)

    def body(count):
        query = rows(own_ref, g, 2)
        scores = []
        for m in range(count):
            tile = pairs_ref[g, m]
            key = jnp.concatenate([rows(own_ref, tile, 0), rows(sib_ref, tile, 0)], axis=0)
            scores.append(
                lax.dot_general(
                    query, key, (((1,), (1,)), ((), ())), preferred_element_type=jnp.float32
                )
            )
        peak = functools.reduce(jnp.maximum, [jnp.max(s, axis=-1, keepdims=True) for s in scores])
        total = jnp.zeros((tile_half, 1), jnp.float32)
        out = jnp.zeros((tile_half, HEAD_DIM), jnp.float32)
        for m in range(count):
            tile = pairs_ref[g, m]
            value = jnp.concatenate([rows(own_ref, tile, 1), rows(sib_ref, tile, 1)], axis=0)
            exps = jnp.exp2((scores[m] - peak) * factor)
            total = total + jnp.sum(exps, axis=-1, keepdims=True)
            out = out + jnp.dot(
                exps.astype(jnp.bfloat16), value, preferred_element_type=jnp.float32
            )
        out = (out / total).astype(o_ref.dtype)
        o_ref[...] = out.reshape(sources, half, HEAD_DIM)

    full = pairs_ref[g, MAXK] > MAXK - 1

    @pl.when(full)
    def _():
        body(MAXK)

    @pl.when(jnp.logical_not(full))
    def _():
        body(MAXK - 1)


def local(queries, keys, values, pairs, pair_count):
    axes = ("seq", "head")
    devices = lax.axis_size("seq") * lax.axis_size("head")
    head_size = lax.axis_size("head")
    tokens, width = queries.shape
    half = tokens // CORES
    heads = width // HEAD_DIM
    chips_used = heads // head_size
    group = CORES * head_size
    own_tiles = pairs.shape[0]
    tiles = own_tiles * lax.axis_size("seq")
    sources = devices // tiles

    table = jnp.concatenate([pairs, pair_count[:, None]], axis=1)
    table = lax.all_gather(table, "seq", axis=0, tiled=True)

    packed = pl.pallas_call(
        pack_kernel,
        grid=(chips_used,),
        in_specs=[pl.BlockSpec((tokens, head_size * HEAD_DIM), lambda i: (0, i))] * 3,
        out_specs=pl.BlockSpec((group, 3 * half, HEAD_DIM), lambda i: (i, 0, 0)),
        out_shape=jax.ShapeDtypeStruct((devices, 3 * half, HEAD_DIM), jnp.bfloat16),
        name="pack",
    )(queries, keys, values)
    own = lax.all_to_all(packed, axes, split_axis=0, concat_axis=0, tiled=True)
    swap = [(i, i ^ 1) for i in range(lax.axis_size("seq"))]
    sib = lax.ppermute(own, "seq", swap)

    flops = 4 * tiles * sources * half * MAXK * sources * tokens * HEAD_DIM
    whole = pl.BlockSpec((devices, 3 * half, HEAD_DIM), lambda g, table: (0, 0, 0))
    attended = pl.pallas_call(
        functools.partial(attend_kernel, sources=sources, half=half),
        grid_spec=pltpu.PrefetchScalarGridSpec(
            num_scalar_prefetch=1,
            grid=(tiles,),
            in_specs=[whole, whole],
            out_specs=pl.BlockSpec((sources, half, HEAD_DIM), lambda g, table: (g, 0, 0)),
        ),
        out_shape=jax.ShapeDtypeStruct((devices, half, HEAD_DIM), jnp.bfloat16),
        compiler_params=pltpu.CompilerParams(vmem_limit_bytes=56 * MIB),
        cost_estimate=pl.CostEstimate(
            flops=flops, bytes_accessed=12 * MIB, transcendentals=flops // (4 * HEAD_DIM)
        ),
        name="attend",
    )(table, own, sib)

    back = lax.all_to_all(attended, axes, split_axis=0, concat_axis=0, tiled=True)
    return pl.pallas_call(
        unpack_kernel,
        grid=(chips_used,),
        in_specs=[pl.BlockSpec((group, half, HEAD_DIM), lambda i: (i, 0, 0))],
        out_specs=pl.BlockSpec((tokens, head_size * HEAD_DIM), lambda i: (0, i)),
        out_shape=jax.ShapeDtypeStruct((tokens, width), jnp.bfloat16),
        name="unpack",
    )(back)


def solution(mesh):
    placed = (
        P(("seq", "head"), None),
        P(("seq", "head"), None),
        P(("seq", "head"), None),
        P("seq", None),
        P("seq"),
    )
    return jax.shard_map(
        local, mesh=mesh, in_specs=placed, out_specs=P(("seq", "head"), None), check_vma=False
    )
```

```python
import functools
import math

import jax
import jax.numpy as jnp
from jax import lax
from jax.experimental import pallas as pl
from jax.experimental.pallas import tpu as pltpu
from jax.sharding import PartitionSpec as P

HEAD_DIM = 128
GRID_H = 4
MAXK = 4
CORES = 2
UNROLL = 2
MIB = 1 << 20


def pack_kernel(q_ref, k_ref, v_ref, o_ref):
    half = q_ref.shape[0] // CORES
    heads = q_ref.shape[1] // HEAD_DIM
    for core in range(CORES):
        rows = pl.ds(core * half, half)
        for h in range(heads):
            cols = pl.ds(h * HEAD_DIM, HEAD_DIM)
            for part, ref in enumerate((k_ref, v_ref, q_ref)):
                o_ref[core * heads + h, pl.ds(part * half, half), :] = ref[rows, cols]


def unpack_kernel(i_ref, o_ref):
    half = i_ref.shape[1]
    heads = i_ref.shape[0] // CORES
    for core in range(CORES):
        for h in range(heads):
            o_ref[pl.ds(core * half, half), pl.ds(h * HEAD_DIM, HEAD_DIM)] = i_ref[core * heads + h]


def attend_kernel(*refs, sources, half, slabs):
    where, parts = refs[0], refs[1 : 1 + slabs]
    own_hbm, sib_hbm, o_ref, own, sib, table, order, sems = refs[1 + slabs :]
    tile_half = sources * half
    tiles = own.shape[0] // sources
    slab_len = own.shape[0] // slabs
    slab_tiles = tiles // slabs
    row_tiles = slab_tiles // GRID_H
    factor = math.log2(math.e) / math.sqrt(HEAD_DIM)

    def copies(slab):
        at = pl.ds(slab * slab_len, slab_len)
        return (
            pltpu.make_async_copy(own_hbm.at[at], own.at[at], sems.at[0, slab]),
            pltpu.make_async_copy(
                sib_hbm.at[at, pl.ds(0, 2 * half)], sib.at[at], sems.at[1, slab]
            ),
        )

    for slab in range(slabs):
        for copy in copies(slab):
            copy.start()

    my_slab, my_row = where[0] // GRID_H, where[0] % GRID_H
    for e in range(slabs):
        for d in range(GRID_H):
            row = (my_slab + slabs - e) % slabs * GRID_H + (my_row + GRID_H - d) % GRID_H
            for w in range(row_tiles):
                for m in range(MAXK):
                    table[row * row_tiles + w, m] = parts[e][d, w * MAXK + m]
                table[row * row_tiles + w, MAXK] = parts[e][d, row_tiles * MAXK + w]

    def sort(g, filled):
        full = table[g, MAXK] > MAXK - 1
        n_full, n_less = filled

        @pl.when(full)
        def _():
            order[0, n_full] = g

        @pl.when(jnp.logical_not(full))
        def _():
            order[1, n_less] = g

        step = full.astype(jnp.int32)
        return n_full + step, n_less + 1 - step

    filled = lax.fori_loop(0, tiles, sort, (jnp.int32(0), jnp.int32(0)))

    def rows(ref, tile, part):
        block = ref[pl.ds(tile * sources, sources), pl.ds(part * half, half), :]
        return block.reshape(tile_half, HEAD_DIM)

    def both(tile, part):
        return jnp.concatenate([rows(own, tile, part), rows(sib, tile, part)], axis=0)

    def attend(g, count):
        query = rows(own, g, 2)
        scores = [
            lax.dot_general(
                query,
                both(table[g, m], 0),
                (((1,), (1,)), ((), ())),
                preferred_element_type=jnp.float32,
            )
            for m in range(count)
        ]
        peak = jnp.max(functools.reduce(jnp.maximum, scores), axis=-1, keepdims=True)
        out = jnp.zeros((tile_half, 2 * HEAD_DIM), jnp.float32)
        for m in range(count):
            probs = jnp.exp2((scores[m] - peak) * factor).astype(jnp.bfloat16)
            value = both(table[g, m], 1)
            value = jnp.concatenate([value, jnp.ones_like(value)], axis=1)
            out = out + jnp.dot(probs, value, preferred_element_type=jnp.float32)
        return out[:, :HEAD_DIM] / out[:, HEAD_DIM:]

    def loaded(have, need):
        for slab in range(slabs):

            @pl.when(jnp.logical_and(have <= slab, slab < need))
            def _(slab=slab):
                for copy in copies(slab):
                    copy.wait()

        return jnp.maximum(have, need)

    have = jnp.int32(0)
    for kind, count in enumerate((MAXK, MAXK - 1)):
        number = filled[kind]

        def step(i, have, kind=kind, count=count, number=number):
            picked = [
                order[kind, jnp.minimum(i * UNROLL + u, number - 1)] for u in range(UNROLL)
            ]
            have = loaded(have, jnp.minimum(picked[-1] // slab_tiles + 2, slabs))
            outs = [attend(g, count) for g in picked]
            for g, out in zip(picked, outs):
                o_ref[pl.ds(g * sources, sources)] = out.astype(o_ref.dtype).reshape(
                    sources, half, HEAD_DIM
                )
            return have

        have = lax.fori_loop(0, (number + UNROLL - 1) // UNROLL, step, have)
    loaded(have, slabs)


def local(queries, keys, values, pairs, pair_count):
    axes = ("seq", "head")
    rows_all = lax.axis_size("seq")
    devices = rows_all * lax.axis_size("head")
    head_size = lax.axis_size("head")
    tokens, width = queries.shape
    half = tokens // CORES
    heads = width // HEAD_DIM
    chips_used = heads // head_size
    group = CORES * head_size
    own_tiles = pairs.shape[0]
    tiles = own_tiles * rows_all
    sources = devices // tiles
    slabs = rows_all // GRID_H

    entry = jnp.concatenate([pairs.reshape(1, -1), pair_count.reshape(1, -1)], axis=1)
    in_slab = [entry] + [
        lax.ppermute(
            entry,
            "seq",
            [(s, s // GRID_H * GRID_H + (s + d) % GRID_H) for s in range(rows_all)],
        )
        for d in range(1, GRID_H)
    ]
    in_slab = jnp.concatenate(in_slab, axis=0)

    packed = pl.pallas_call(
        pack_kernel,
        grid=(chips_used,),
        in_specs=[pl.BlockSpec((tokens, head_size * HEAD_DIM), lambda i: (0, i))] * 3,
        out_specs=pl.BlockSpec((group, 3 * half, HEAD_DIM), lambda i: (i, 0, 0)),
        out_shape=jax.ShapeDtypeStruct((devices, 3 * half, HEAD_DIM), jnp.bfloat16),
        name="pack",
    )(queries, keys, values)
    own = lax.all_to_all(packed, axes, split_axis=0, concat_axis=0, tiled=True)
    sib = lax.ppermute(own, "seq", [(s, s ^ 1) for s in range(rows_all)])
    in_slab, own = lax.optimization_barrier((in_slab, own))
    parts = [in_slab] + [
        lax.ppermute(in_slab, "seq", [(s, (s + e * GRID_H) % rows_all) for s in range(rows_all)])
        for e in range(1, slabs)
    ]
    where = lax.axis_index("seq").astype(jnp.int32).reshape(1)

    flops = 4 * tiles * sources * half * MAXK * sources * tokens * HEAD_DIM
    anywhere = pl.BlockSpec(memory_space=pl.ANY)
    attended = pl.pallas_call(
        functools.partial(attend_kernel, sources=sources, half=half, slabs=slabs),
        grid_spec=pltpu.PrefetchScalarGridSpec(
            num_scalar_prefetch=1 + slabs,
            grid=(1,),
            in_specs=[anywhere, anywhere],
            out_specs=pl.BlockSpec((devices, half, HEAD_DIM), lambda i, *_: (0, 0, 0)),
            scratch_shapes=[
                pltpu.VMEM((devices, 3 * half, HEAD_DIM), jnp.bfloat16),
                pltpu.VMEM((devices, 2 * half, HEAD_DIM), jnp.bfloat16),
                pltpu.SMEM((tiles, MAXK + 1), jnp.int32),
                pltpu.SMEM((2, tiles), jnp.int32),
                pltpu.SemaphoreType.DMA((2, slabs)),
            ],
        ),
        out_shape=jax.ShapeDtypeStruct((devices, half, HEAD_DIM), jnp.bfloat16),
        compiler_params=pltpu.CompilerParams(vmem_limit_bytes=48 * MIB),
        cost_estimate=pl.CostEstimate(
            flops=flops, bytes_accessed=12 * MIB, transcendentals=flops // (4 * HEAD_DIM)
        ),
        name="attend",
    )(where, *parts, own, sib)

    back = lax.all_to_all(attended, axes, split_axis=0, concat_axis=0, tiled=True)
    return pl.pallas_call(
        unpack_kernel,
        grid=(chips_used,),
        in_specs=[pl.BlockSpec((group, half, HEAD_DIM), lambda i: (i, 0, 0))],
        out_specs=pl.BlockSpec((tokens, head_size * HEAD_DIM), lambda i: (0, i)),
        out_shape=jax.ShapeDtypeStruct((tokens, width), jnp.bfloat16),
        name="unpack",
    )(back)


def solution(mesh):
    placed = (
        P(("seq", "head"), None),
        P(("seq", "head"), None),
        P(("seq", "head"), None),
        P("seq", None),
        P("seq"),
    )
    return jax.shard_map(
        local, mesh=mesh, in_specs=placed, out_specs=P(("seq", "head"), None), check_vma=False
    )
```

```python
import functools
import math

import jax
import jax.numpy as jnp
from jax import lax
from jax.experimental import pallas as pl
from jax.experimental.pallas import tpu as pltpu
from jax.sharding import PartitionSpec as P

HEAD_DIM = 128
GRID_H = 4
MAXK = 4
CORES = 2
UNROLL = 2
MIB = 1 << 20


def pack_kernel(q_ref, k_ref, v_ref, o_ref):
    half = q_ref.shape[0] // CORES
    heads = q_ref.shape[1] // HEAD_DIM
    for core in range(CORES):
        rows = pl.ds(core * half, half)
        for h in range(heads):
            cols = pl.ds(h * HEAD_DIM, HEAD_DIM)
            for part, ref in enumerate((k_ref, v_ref, q_ref)):
                o_ref[core * heads + h, pl.ds(part * half, half), :] = ref[rows, cols]


def attend_kernel(*refs, sources, half, slabs):
    where, parts = refs[0], refs[1 : 1 + slabs]
    own_hbm, sib_hbm, o_ref, own, sib, table, order, sems = refs[1 + slabs :]
    tile_half = sources * half
    tiles = own.shape[0] // sources
    slab_len = own.shape[0] // slabs
    slab_tiles = tiles // slabs
    row_tiles = slab_tiles // GRID_H
    factor = math.log2(math.e) / math.sqrt(HEAD_DIM)

    def copies(slab):
        at = pl.ds(slab * slab_len, slab_len)
        return (
            pltpu.make_async_copy(own_hbm.at[at], own.at[at], sems.at[0, slab]),
            pltpu.make_async_copy(
                sib_hbm.at[at, pl.ds(0, 2 * half)], sib.at[at], sems.at[1, slab]
            ),
        )

    for slab in range(slabs):
        for copy in copies(slab):
            copy.start()

    my_slab, my_row = where[0] // GRID_H, where[0] % GRID_H
    for e in range(slabs):
        for d in range(GRID_H):
            row = (my_slab + slabs - e) % slabs * GRID_H + (my_row + GRID_H - d) % GRID_H
            for w in range(row_tiles):
                for m in range(MAXK):
                    table[row * row_tiles + w, m] = parts[e][d, w * MAXK + m]
                table[row * row_tiles + w, MAXK] = parts[e][d, row_tiles * MAXK + w]

    def sort(g, filled):
        full = table[g, MAXK] > MAXK - 1
        n_full, n_less = filled

        @pl.when(full)
        def _():
            order[0, n_full] = g

        @pl.when(jnp.logical_not(full))
        def _():
            order[1, n_less] = g

        step = full.astype(jnp.int32)
        return n_full + step, n_less + 1 - step

    filled = lax.fori_loop(0, tiles, sort, (jnp.int32(0), jnp.int32(0)))

    def rows(ref, tile, part):
        block = ref[pl.ds(tile * sources, sources), pl.ds(part * half, half), :]
        return block.reshape(tile_half, HEAD_DIM)

    def both(tile, part):
        return jnp.concatenate([rows(own, tile, part), rows(sib, tile, part)], axis=0)

    def attend(g, count):
        query = rows(own, g, 2)
        scores = [
            lax.dot_general(
                query,
                both(table[g, m], 0),
                (((1,), (1,)), ((), ())),
                preferred_element_type=jnp.float32,
            )
            for m in range(count)
        ]
        peak = jnp.max(functools.reduce(jnp.maximum, scores), axis=-1, keepdims=True)
        out = jnp.zeros((tile_half, 2 * HEAD_DIM), jnp.float32)
        for m in range(count):
            probs = jnp.exp2((scores[m] - peak) * factor).astype(jnp.bfloat16)
            value = both(table[g, m], 1)
            value = jnp.concatenate([value, jnp.ones_like(value)], axis=1)
            out = out + jnp.dot(probs, value, preferred_element_type=jnp.float32)
        return out[:, :HEAD_DIM] / out[:, HEAD_DIM:]

    def loaded(have, need):
        for slab in range(slabs):

            @pl.when(jnp.logical_and(have <= slab, slab < need))
            def _(slab=slab):
                for copy in copies(slab):
                    copy.wait()

        return jnp.maximum(have, need)

    have = jnp.int32(0)
    for kind, count in enumerate((MAXK, MAXK - 1)):
        number = filled[kind]

        def step(i, have, kind=kind, count=count, number=number):
            picked = [
                order[kind, jnp.minimum(i * UNROLL + u, number - 1)] for u in range(UNROLL)
            ]
            have = loaded(have, jnp.minimum(picked[-1] // slab_tiles + 2, slabs))
            outs = [attend(g, count) for g in picked]
            for g, out in zip(picked, outs):
                o_ref[pl.ds(g * sources, sources)] = out.astype(o_ref.dtype).reshape(
                    sources, half, HEAD_DIM
                )
            return have

        have = lax.fori_loop(0, (number + UNROLL - 1) // UNROLL, step, have)
    loaded(have, slabs)


def local(queries, keys, values, pairs, pair_count):
    axes = ("seq", "head")
    rows_all = lax.axis_size("seq")
    devices = rows_all * lax.axis_size("head")
    head_size = lax.axis_size("head")
    tokens, width = queries.shape
    half = tokens // CORES
    heads = width // HEAD_DIM
    chips_used = heads // head_size
    group = CORES * head_size
    own_tiles = pairs.shape[0]
    tiles = own_tiles * rows_all
    sources = devices // tiles
    slabs = rows_all // GRID_H

    entry = jnp.concatenate([pairs.reshape(1, -1), pair_count.reshape(1, -1)], axis=1)
    in_slab = [entry] + [
        lax.ppermute(
            entry,
            "seq",
            [(s, s // GRID_H * GRID_H + (s + d) % GRID_H) for s in range(rows_all)],
        )
        for d in range(1, GRID_H)
    ]
    in_slab = jnp.concatenate(in_slab, axis=0)

    packed = pl.pallas_call(
        pack_kernel,
        grid=(chips_used,),
        in_specs=[pl.BlockSpec((tokens, head_size * HEAD_DIM), lambda i: (0, i))] * 3,
        out_specs=pl.BlockSpec((group, 3 * half, HEAD_DIM), lambda i: (i, 0, 0)),
        out_shape=jax.ShapeDtypeStruct((devices, 3 * half, HEAD_DIM), jnp.bfloat16),
        cost_estimate=pl.CostEstimate(flops=0, bytes_accessed=6 * MIB, transcendentals=0),
        name="pack",
    )(queries, keys, values)
    in_slab, packed = lax.optimization_barrier((in_slab, packed))
    own = lax.all_to_all(packed, axes, split_axis=0, concat_axis=0, tiled=True)
    sib = lax.ppermute(own, "seq", [(s, s ^ 1) for s in range(rows_all)])
    in_slab, own = lax.optimization_barrier((in_slab, own))
    parts = [in_slab] + [
        lax.ppermute(in_slab, "seq", [(s, (s + e * GRID_H) % rows_all) for s in range(rows_all)])
        for e in range(1, slabs)
    ]
    where = lax.axis_index("seq").astype(jnp.int32).reshape(1)

    flops = 4 * tiles * sources * half * MAXK * sources * tokens * HEAD_DIM
    anywhere = pl.BlockSpec(memory_space=pl.ANY)
    attended = pl.pallas_call(
        functools.partial(attend_kernel, sources=sources, half=half, slabs=slabs),
        grid_spec=pltpu.PrefetchScalarGridSpec(
            num_scalar_prefetch=1 + slabs,
            grid=(1,),
            in_specs=[anywhere, anywhere],
            out_specs=pl.BlockSpec((devices, half, HEAD_DIM), lambda i, *_: (0, 0, 0)),
            scratch_shapes=[
                pltpu.VMEM((devices, 3 * half, HEAD_DIM), jnp.bfloat16),
                pltpu.VMEM((devices, 2 * half, HEAD_DIM), jnp.bfloat16),
                pltpu.SMEM((tiles, MAXK + 1), jnp.int32),
                pltpu.SMEM((2, tiles), jnp.int32),
                pltpu.SemaphoreType.DMA((2, slabs)),
            ],
        ),
        out_shape=jax.ShapeDtypeStruct((devices, half, HEAD_DIM), jnp.bfloat16),
        compiler_params=pltpu.CompilerParams(vmem_limit_bytes=48 * MIB),
        cost_estimate=pl.CostEstimate(
            flops=flops, bytes_accessed=12 * MIB, transcendentals=flops // (4 * HEAD_DIM)
        ),
        name="attend",
    )(where, *parts, own, sib)

    back = lax.all_to_all(attended, axes, split_axis=0, concat_axis=0, tiled=True)
    back = back.reshape(-1, CORES, head_size, half, HEAD_DIM)[:chips_used]
    return back.transpose(1, 3, 0, 2, 4).reshape(tokens, width)


def solution(mesh):
    placed = (
        P(("seq", "head"), None),
        P(("seq", "head"), None),
        P(("seq", "head"), None),
        P("seq", None),
        P("seq"),
    )
    return jax.shard_map(
        local, mesh=mesh, in_specs=placed, out_specs=P(("seq", "head"), None), check_vma=False
    )
```

```python
import functools
import math

import jax
import jax.numpy as jnp
from jax import lax
from jax.experimental import pallas as pl
from jax.experimental.pallas import tpu as pltpu
from jax.sharding import PartitionSpec as P

HEAD_DIM = 128
GRID_H = 4
MAXK = 4
CORES = 2
MIB = 1 << 20


def pack_kernel(q_ref, k_ref, v_ref, o_ref):
    tokens, width = q_ref.shape
    for h in range(width // HEAD_DIM):
        cols = pl.ds(h * HEAD_DIM, HEAD_DIM)
        for part, ref in enumerate((k_ref, v_ref, q_ref)):
            o_ref[h, pl.ds(part * tokens, tokens), :] = ref[:, cols]


def attend_kernel(*refs, sources, slabs):
    where, parts = refs[0], refs[1 : 1 + slabs]
    own_hbm, sib_hbm, o_hbm = refs[1 + slabs : 4 + slabs]
    kv, queries, outs, scores, peaks, table, order, in_sems, out_sems = refs[4 + slabs :]
    tokens = queries.shape[1]
    tile_len = sources * tokens
    tiles = queries.shape[0] // sources
    slab_len = queries.shape[0] // slabs
    slab_tiles = tiles // slabs
    row_tiles = table.shape[0] // (slabs * GRID_H)
    row_len = row_tiles * sources
    core = where[0] % CORES
    factor = math.log2(math.e) / math.sqrt(HEAD_DIM)

    def copies(slab):
        at = pl.ds(slab * slab_len, slab_len)
        keys = pl.ds(0, 2 * tokens)
        return (
            pltpu.make_async_copy(
                own_hbm.at[at, pl.ds(2 * tokens, tokens)], queries.at[at], in_sems.at[0, slab]
            ),
            pltpu.make_async_copy(own_hbm.at[at, keys], kv.at[0, at], in_sems.at[1, slab]),
            pltpu.make_async_copy(sib_hbm.at[at, keys], kv.at[1, at], in_sems.at[2, slab]),
        )

    for slab in range(slabs):
        for copy in copies(slab):
            copy.start()

    my_slab, my_row = where[0] // GRID_H, where[0] % GRID_H
    for e in range(slabs):
        for d in range(GRID_H):
            row = (my_slab + slabs - e) % slabs * GRID_H + (my_row + GRID_H - d) % GRID_H
            for w in range(row_tiles):
                for m in range(MAXK):
                    table[row * row_tiles + w, m] = parts[e][d, w * MAXK + m]
                table[row * row_tiles + w, MAXK] = parts[e][d, row_tiles * MAXK + w]

    def whole(local):
        return (local // row_tiles * CORES + core) * row_tiles + local % row_tiles

    def sort(local, filled):
        full = table[whole(local), MAXK] > MAXK - 1
        n_full, n_less = filled

        @pl.when(full)
        def _():
            order[0, n_full] = local

        @pl.when(jnp.logical_not(full))
        def _():
            order[1, n_less] = local

        step = full.astype(jnp.int32)
        return n_full + step, n_less + 1 - step

    filled = lax.fori_loop(0, tiles, sort, (jnp.int32(0), jnp.int32(0)))

    def loaded(have, need):
        for slab in range(slabs):

            @pl.when(jnp.logical_and(have <= slab, slab < need))
            def _(slab=slab):
                for copy in copies(slab):
                    copy.wait()

        return jnp.maximum(have, need)

    def listed(local, m, part):
        tile = table[whole(local), m]
        row = tile // row_tiles
        side = (row + core) % CORES
        first = row // CORES * row_len + tile % row_tiles * sources
        block = kv[side, pl.ds(first, sources), pl.ds(part * tokens, tokens), :]
        return block.reshape(tile_len, HEAD_DIM)

    def query_of(local):
        return queries[pl.ds(local * sources, sources)].reshape(tile_len, HEAD_DIM)

    def score(local, slot, m, query, peak):
        block = lax.dot_general(
            query, listed(local, m, 0), (((1,), (1,)), ((), ())), preferred_element_type=jnp.float32
        )
        scores[slot, m] = block
        for at in range(0, tile_len, HEAD_DIM):
            part = block[:, at : at + HEAD_DIM]
            peak = part if peak is None else jnp.maximum(peak, part)
        return peak

    def keep_peak(slot, peak):
        peaks[slot] = jnp.broadcast_to(jnp.max(peak, axis=-1, keepdims=True), peak.shape)

    def weigh(local, slot, m, peak, total):
        probs = jnp.exp2((scores[slot, m] - peak) * factor).astype(jnp.bfloat16)
        value = listed(local, m, 1)
        value = jnp.concatenate([value, jnp.ones_like(value)], axis=1)
        return total + jnp.dot(probs, value, preferred_element_type=jnp.float32)

    def sent(local):
        at = pl.ds(local * sources, sources)
        return pltpu.make_async_copy(outs.at[at], o_hbm.at[at], out_sems.at[local])

    def pair(this, this_slot, then, then_slot, count, fresh):
        total = jnp.zeros((tile_len, 2 * HEAD_DIM), jnp.float32)
        peak = jnp.concatenate([peaks[this_slot]] * (tile_len // HEAD_DIM), axis=1)
        query, then_peak = query_of(then), None
        for m in range(count):
            then_peak = score(then, then_slot, m, query, then_peak)
            total = weigh(this, this_slot, m, peak, total)
        keep_peak(then_slot, then_peak)
        out = (total[:, :HEAD_DIM] / total[:, HEAD_DIM:]).astype(outs.dtype)
        place = this if fresh is None else jnp.where(fresh, this, tiles)
        outs[pl.ds(place * sources, sources)] = out.reshape(sources, tokens, HEAD_DIM)
        if fresh is None:
            sent(this).start()
        else:
            pl.when(fresh)(lambda: sent(this).start())

    def need(local):
        return jnp.minimum(local // slab_tiles + 2, slabs)

    have = jnp.int32(0)
    for kind, count in enumerate((MAXK, MAXK - 1)):
        number = filled[kind]

        def pick(i, kind=kind, number=number):
            return order[kind, jnp.minimum(i, number - 1)]

        def first(have, count=count, pick=pick):
            local = pick(0)
            have = loaded(have, need(local))
            query, peak = query_of(local), None
            for m in range(count):
                peak = score(local, 0, m, query, peak)
            keep_peak(0, peak)
            return have

        have = lax.cond(number > 0, first, lambda have: have, have)

        def step(i, have, count=count, pick=pick, number=number):
            a, b, c = pick(2 * i), pick(2 * i + 1), pick(2 * i + 2)
            have = loaded(have, need(c))
            pair(a, 0, b, 1, count, None)
            pair(b, 1, c, 0, count, 2 * i + 1 < number)
            return have

        have = lax.fori_loop(0, (number + 1) // 2, step, have)
    loaded(have, slabs)
    for local in range(tiles):
        sent(local).wait()


def local(queries, keys, values, pairs, pair_count):
    axes = ("seq", "head")
    rows_all = lax.axis_size("seq")
    head_size = lax.axis_size("head")
    devices = rows_all * head_size
    tokens, width = queries.shape
    heads = width // HEAD_DIM
    row_tiles = pairs.shape[0]
    tiles = row_tiles * rows_all
    sources = devices // tiles
    slabs = rows_all // GRID_H
    chips = devices // CORES
    same_core = [
        [s * head_size + h for s in range(core, rows_all, CORES) for h in range(head_size)]
        for core in range(CORES)
    ]

    entry = jnp.concatenate([pairs.reshape(1, -1), pair_count.reshape(1, -1)], axis=1)
    in_slab = [entry] + [
        lax.ppermute(
            entry,
            "seq",
            [(s, s // GRID_H * GRID_H + (s + d) % GRID_H) for s in range(rows_all)],
        )
        for d in range(1, GRID_H)
    ]
    in_slab = jnp.concatenate(in_slab, axis=0)

    packed = pl.pallas_call(
        pack_kernel,
        grid=(heads // head_size,),
        in_specs=[pl.BlockSpec((tokens, head_size * HEAD_DIM), lambda i: (0, i))] * 3,
        out_specs=pl.BlockSpec((head_size, 3 * tokens, HEAD_DIM), lambda i: (i, 0, 0)),
        out_shape=jax.ShapeDtypeStruct((chips, 3 * tokens, HEAD_DIM), jnp.bfloat16),
        cost_estimate=pl.CostEstimate(flops=0, bytes_accessed=6 * MIB, transcendentals=0),
        name="pack",
    )(queries, keys, values)
    in_slab, packed = lax.optimization_barrier((in_slab, packed))
    own = lax.all_to_all(
        packed, axes, split_axis=0, concat_axis=0, tiled=True, axis_index_groups=same_core
    )
    sib = lax.ppermute(own, "seq", [(s, s ^ 1) for s in range(rows_all)])
    in_slab, own = lax.optimization_barrier((in_slab, own))
    parts = [in_slab] + [
        lax.ppermute(in_slab, "seq", [(s, (s + e * GRID_H) % rows_all) for s in range(rows_all)])
        for e in range(1, slabs)
    ]
    where = lax.axis_index("seq").astype(jnp.int32).reshape(1)

    tile_len = sources * tokens
    flops = 4 * (tiles // CORES) * tile_len * MAXK * tile_len * HEAD_DIM
    anywhere = pl.BlockSpec(memory_space=pl.ANY)
    attended = pl.pallas_call(
        functools.partial(attend_kernel, sources=sources, slabs=slabs),
        grid_spec=pltpu.PrefetchScalarGridSpec(
            num_scalar_prefetch=1 + slabs,
            grid=(1,),
            in_specs=[anywhere, anywhere],
            out_specs=anywhere,
            scratch_shapes=[
                pltpu.VMEM((CORES, chips, 2 * tokens, HEAD_DIM), jnp.bfloat16),
                pltpu.VMEM((chips, tokens, HEAD_DIM), jnp.bfloat16),
                pltpu.VMEM((chips + sources, tokens, HEAD_DIM), jnp.bfloat16),
                pltpu.VMEM((2, MAXK, tile_len, tile_len), jnp.float32),
                pltpu.VMEM((2, tile_len, HEAD_DIM), jnp.float32),
                pltpu.SMEM((tiles, MAXK + 1), jnp.int32),
                pltpu.SMEM((2, tiles // CORES), jnp.int32),
                pltpu.SemaphoreType.DMA((3, slabs)),
                pltpu.SemaphoreType.DMA((tiles // CORES,)),
            ],
        ),
        out_shape=jax.ShapeDtypeStruct((chips, tokens, HEAD_DIM), jnp.bfloat16),
        compiler_params=pltpu.CompilerParams(vmem_limit_bytes=48 * MIB),
        cost_estimate=pl.CostEstimate(
            flops=flops, bytes_accessed=12 * MIB, transcendentals=flops // (4 * HEAD_DIM)
        ),
        name="attend",
    )(where, *parts, own, sib)

    back = lax.all_to_all(
        attended, axes, split_axis=0, concat_axis=0, tiled=True, axis_index_groups=same_core
    )
    return back[:heads].transpose(1, 0, 2).reshape(tokens, width)


def solution(mesh):
    placed = (
        P(("seq", "head"), None),
        P(("seq", "head"), None),
        P(("seq", "head"), None),
        P("seq", None),
        P("seq"),
    )
    return jax.shard_map(
        local, mesh=mesh, in_specs=placed, out_specs=P(("seq", "head"), None), check_vma=False
    )
```

```python
import functools
import math

import jax
import jax.numpy as jnp
from jax import lax
from jax.experimental import pallas as pl
from jax.experimental.pallas import tpu as pltpu
from jax.sharding import PartitionSpec as P

HEAD_DIM = 128
GRID_H = 4
MAXK = 4
CORES = 2
TABLE_ROWS = 16
PACK_STEPS = 2
MIB = 1 << 20


def pack_kernel(q_ref, k_ref, v_ref, pairs_ref, count_ref, o_ref, table):
    tokens, width = q_ref.shape
    row_tiles = pairs_ref.shape[0]
    table[...] = jnp.zeros_like(table)
    table[pl.ds(0, row_tiles), pl.ds(0, MAXK)] = pairs_ref[...].astype(jnp.float32)
    table[pl.ds(row_tiles, 1), pl.ds(0, row_tiles)] = count_ref[...].astype(jnp.float32)
    for h in range(width // HEAD_DIM):
        cols = pl.ds(h * HEAD_DIM, HEAD_DIM)
        for part, ref in enumerate((k_ref, v_ref, q_ref)):
            o_ref[h, pl.ds(part * tokens, tokens), :] = ref[:, cols]
        o_ref[h, pl.ds(3 * tokens, TABLE_ROWS), :] = table[...].astype(jnp.bfloat16)


def attend_kernel(own_hbm, sib_hbm, o_hbm, *scratch, row_len, row_tiles, slabs):
    kv, queries, outs, scores, peaks, totals, rows_in, rows_int, table, place, order = scratch[:11]
    in_sems, out_sems, row_sems, table_sem = scratch[11:]
    chips, tokens, _ = queries.shape
    sources = row_len // row_tiles
    tile_len = sources * tokens
    tiles = chips // sources
    slab_len = chips // slabs
    slab_tiles = tiles // slabs
    core = lax.axis_index("seq") % CORES
    factor = math.log2(math.e) / math.sqrt(HEAD_DIM)

    def copies(slab):
        at = pl.ds(slab * slab_len, slab_len)
        beside = pl.ds(chips + slab * slab_len, slab_len)
        return (
            pltpu.make_async_copy(
                own_hbm.at[at, pl.ds(2 * tokens, tokens)], queries.at[at], in_sems.at[0, slab]
            ),
            pltpu.make_async_copy(
                own_hbm.at[at, pl.ds(0, 2 * tokens)], kv.at[at], in_sems.at[1, slab]
            ),
            pltpu.make_async_copy(sib_hbm.at[at], kv.at[beside], in_sems.at[2, slab]),
        )

    fetches = [
        pltpu.make_async_copy(
            own_hbm.at[row * row_len, pl.ds(3 * tokens, TABLE_ROWS)],
            rows_in.at[row],
            row_sems.at[row],
        )
        for row in range(chips // row_len)
    ]
    for fetch in fetches:
        fetch.start()
    for slab in range(2):
        for copy in copies(slab):
            copy.start()
    for fetch in fetches:
        fetch.wait()
    rows_int[...] = rows_in[...].astype(jnp.float32)[:, : rows_int.shape[1]].astype(jnp.int32)
    spread = pltpu.make_async_copy(rows_int, table, table_sem.at[0])
    spread.start()
    spread.wait()

    def sort(local, filled):
        at, w = local // row_tiles, local % row_tiles
        for m in range(MAXK):
            tile = jnp.clip(table[at, w, m], 0, CORES * tiles - 1)
            row = tile // row_tiles
            side = (row + core) % CORES
            place[local, m] = side * chips + row // CORES * row_len + tile % row_tiles * sources
        full = table[at, row_tiles, w] > MAXK - 1
        n_full, n_less = filled

        @pl.when(full)
        def _():
            order[0, n_full] = local

        @pl.when(jnp.logical_not(full))
        def _():
            order[1, n_less] = local

        step = full.astype(jnp.int32)
        return n_full + step, n_less + 1 - step

    filled = lax.fori_loop(0, tiles, sort, (jnp.int32(0), jnp.int32(0)))

    def loaded(have, need):
        for slab in range(slabs):

            @pl.when(jnp.logical_and(have <= slab, slab < need))
            def _(slab=slab):
                for copy in copies(slab):
                    copy.wait()

        return jnp.maximum(have, need)

    def listed(local, m, part):
        block = kv[pl.ds(place[local, m], sources), pl.ds(part * tokens, tokens), :]
        return block.reshape(tile_len, HEAD_DIM)

    def query_of(local):
        return queries[pl.ds(local * sources, sources)].reshape(tile_len, HEAD_DIM)

    def score(local, m, query, peak):
        block = lax.dot_general(
            query, listed(local, m, 0), (((1,), (1,)), ((), ())), preferred_element_type=jnp.float32
        )
        scores[m] = block
        for at in range(0, tile_len, HEAD_DIM):
            part = block[:, at : at + HEAD_DIM]
            peak = part if peak is None else jnp.maximum(peak, part)
        return peak

    def weigh(local, m, peak, total):
        probs = jnp.exp2((scores[m] - peak) * factor).astype(jnp.bfloat16)
        value = listed(local, m, 1)
        value = jnp.concatenate([value, jnp.ones_like(value)], axis=1)
        return total + jnp.dot(probs, value, preferred_element_type=jnp.float32)

    def sent(local):
        at = pl.ds(local * sources, sources)
        return pltpu.make_async_copy(outs.at[at], o_hbm.at[at], out_sems.at[local])

    def finish(local):
        out = totals[:, :HEAD_DIM] / totals[:, HEAD_DIM:]
        outs[pl.ds(local * sources, sources)] = out.astype(outs.dtype).reshape(
            sources, tokens, HEAD_DIM
        )

    def pair(before, this, then, count):
        query = query_of(then)
        finish(before)
        peak = jnp.max(peaks[...], axis=-1, keepdims=True)
        peak = jnp.broadcast_to(peak, (tile_len, tile_len))
        total = jnp.zeros((tile_len, 2 * HEAD_DIM), jnp.float32)
        then_peak = None
        for m in range(count):
            total = weigh(this, m, peak, total)
            then_peak = score(then, m, query, then_peak)
        peaks[...] = then_peak
        totals[...] = total

    def need(local):
        return jnp.minimum(local // slab_tiles + 2, slabs)

    have = loaded(jnp.int32(0), 2)
    for slab in range(2, slabs):
        for copy in copies(slab):
            copy.start()
    for kind, count in enumerate((MAXK, MAXK - 1)):
        number = filled[kind]

        def pick(i, kind=kind, number=number):
            return order[kind, jnp.minimum(i, number - 1)]

        def first(have, count=count, pick=pick):
            local = pick(0)
            have = loaded(have, need(local))
            query, peak = query_of(local), None
            for m in range(count):
                peak = score(local, m, query, peak)
            peaks[...] = peak
            return have

        have = lax.cond(number > 0, first, lambda have: have, have)

        def step(i, have, count=count, pick=pick):
            before, this, then = pick(jnp.maximum(i - 1, 0)), pick(i), pick(i + 1)
            have = loaded(have, need(then))
            pair(before, this, then, count)
            pl.when(i > 0)(lambda: sent(before).start())
            return have

        have = lax.fori_loop(0, number, step, have)

        @pl.when(number > 0)
        def _(pick=pick, number=number):
            finish(pick(number - 1))
            sent(pick(number - 1)).start()

    loaded(have, slabs)
    for local in range(tiles):
        sent(local).wait()


def attend_call(own, sib, *, row_len, row_tiles, slabs):
    chips, tokens = own.shape[0], sib.shape[1] // 2
    sources = row_len // row_tiles
    tiles = chips // sources
    tile_len = sources * tokens
    flops = 4 * tiles * tile_len * MAXK * tile_len * HEAD_DIM
    anywhere = pl.BlockSpec(memory_space=pl.ANY)
    return pl.pallas_call(
        functools.partial(attend_kernel, row_len=row_len, row_tiles=row_tiles, slabs=slabs),
        in_specs=[anywhere, anywhere],
        out_specs=anywhere,
        scratch_shapes=[
            pltpu.VMEM((CORES * chips, 2 * tokens, HEAD_DIM), jnp.bfloat16),
            pltpu.VMEM((chips, tokens, HEAD_DIM), jnp.bfloat16),
            pltpu.VMEM((chips, tokens, HEAD_DIM), jnp.bfloat16),
            pltpu.VMEM((MAXK, tile_len, tile_len), jnp.float32),
            pltpu.VMEM((tile_len, HEAD_DIM), jnp.float32),
            pltpu.VMEM((tile_len, 2 * HEAD_DIM), jnp.float32),
            pltpu.VMEM((chips // row_len, TABLE_ROWS, HEAD_DIM), jnp.bfloat16),
            pltpu.VMEM((chips // row_len, 8, HEAD_DIM), jnp.int32),
            pltpu.SMEM((chips // row_len, 8, HEAD_DIM), jnp.int32),
            pltpu.SMEM((tiles, MAXK), jnp.int32),
            pltpu.SMEM((2, tiles), jnp.int32),
            pltpu.SemaphoreType.DMA((3, slabs)),
            pltpu.SemaphoreType.DMA((tiles,)),
            pltpu.SemaphoreType.DMA((chips // row_len,)),
            pltpu.SemaphoreType.DMA((1,)),
        ],
        out_shape=jax.ShapeDtypeStruct((chips, tokens, HEAD_DIM), jnp.bfloat16),
        compiler_params=pltpu.CompilerParams(vmem_limit_bytes=48 * MIB),
        cost_estimate=pl.CostEstimate(
            flops=flops, bytes_accessed=12 * MIB, transcendentals=flops // (4 * HEAD_DIM)
        ),
        name="attend",
    )(own, sib)


def local(queries, keys, values, pairs, pair_count):
    axes = ("seq", "head")
    rows_all = lax.axis_size("seq")
    head_size = lax.axis_size("head")
    tokens, width = queries.shape
    heads = width // HEAD_DIM
    row_tiles = pairs.shape[0]
    chips = rows_all * head_size // CORES
    slot = 3 * tokens + TABLE_ROWS
    same_core = [
        [s * head_size + h for s in range(core, rows_all, CORES) for h in range(head_size)]
        for core in range(CORES)
    ]

    some = heads // PACK_STEPS
    packed = pl.pallas_call(
        pack_kernel,
        grid=(PACK_STEPS,),
        in_specs=[pl.BlockSpec((tokens, some * HEAD_DIM), lambda i: (0, i))] * 3
        + [
            pl.BlockSpec((row_tiles, MAXK), lambda i: (0, 0)),
            pl.BlockSpec((1, row_tiles), lambda i: (0, 0)),
        ],
        out_specs=pl.BlockSpec((some, slot, HEAD_DIM), lambda i: (i, 0, 0)),
        out_shape=jax.ShapeDtypeStruct((chips, slot, HEAD_DIM), jnp.bfloat16),
        scratch_shapes=[pltpu.VMEM((TABLE_ROWS, HEAD_DIM), jnp.float32)],
        compiler_params=pltpu.CompilerParams(vmem_limit_bytes=32 * MIB),
        name="pack",
    )(queries, keys, values, pairs, pair_count.reshape(1, row_tiles))
    own = lax.all_to_all(
        packed, axes, split_axis=0, concat_axis=0, tiled=True, axis_index_groups=same_core
    )
    swap = [(s, s ^ 1) for s in range(rows_all)]
    sib = lax.ppermute(own[:, : 2 * tokens], "seq", swap)
    attended = attend_call(
        own, sib, row_len=head_size, row_tiles=row_tiles, slabs=rows_all // GRID_H
    )
    back = lax.all_to_all(
        attended, axes, split_axis=0, concat_axis=0, tiled=True, axis_index_groups=same_core
    )
    return back[:heads].transpose(1, 0, 2).reshape(tokens, width)


def solution(mesh):
    placed = (
        P(("seq", "head"), None),
        P(("seq", "head"), None),
        P(("seq", "head"), None),
        P("seq", None),
        P("seq"),
    )
    return jax.shard_map(
        local, mesh=mesh, in_specs=placed, out_specs=P(("seq", "head"), None), check_vma=False
    )
```

```python
import functools
import math

import jax
import jax.numpy as jnp
from jax import lax
from jax.experimental import pallas as pl
from jax.experimental.pallas import tpu as pltpu
from jax.sharding import PartitionSpec as P

HEAD_DIM = 128
MAXK = 4
CORES = 2
TABLE_ROWS = 16
PACK_STEPS = 2
MIB = 1 << 20


def pack_kernel(q_ref, k_ref, v_ref, pairs_ref, count_ref, o_ref, table):
    tokens, width = q_ref.shape
    row_tiles = pairs_ref.shape[0]
    table[...] = jnp.zeros_like(table)
    table[pl.ds(0, row_tiles), pl.ds(0, MAXK)] = pairs_ref[...].astype(jnp.float32)
    table[pl.ds(row_tiles, 1), pl.ds(0, row_tiles)] = count_ref[...].astype(jnp.float32)
    for h in range(width // HEAD_DIM):
        cols = pl.ds(h * HEAD_DIM, HEAD_DIM)
        for part, ref in enumerate((k_ref, v_ref, q_ref)):
            o_ref[h, pl.ds(part * tokens, tokens), :] = ref[:, cols]
        o_ref[h, pl.ds(3 * tokens, TABLE_ROWS), :] = table[...].astype(jnp.bfloat16)


def attend_kernel(own, sib, outs, *scratch, row_len, row_tiles):
    kv, scores, peaks, totals, rows_int, table, place, order, table_sem = scratch
    chips, tokens, _ = outs.shape
    sources = row_len // row_tiles
    tile_len = sources * tokens
    tiles = chips // sources
    core = lax.axis_index("seq") % CORES
    factor = math.log2(math.e) / math.sqrt(HEAD_DIM)

    for row in range(chips // row_len):
        block = own[row * row_len, pl.ds(3 * tokens, TABLE_ROWS), :].astype(jnp.float32)
        rows_int[row] = block[: rows_int.shape[1]].astype(jnp.int32)
    spread = pltpu.make_async_copy(rows_int, table, table_sem.at[0])
    spread.start()

    def gather(source, carry):
        kv[source] = own[source, pl.ds(0, 2 * tokens), :]
        kv[chips + source] = sib[source]
        return carry

    lax.fori_loop(0, chips, gather, 0)
    spread.wait()

    def sort(local, filled):
        at, w = local // row_tiles, local % row_tiles
        for m in range(MAXK):
            tile = jnp.clip(table[at, w, m], 0, CORES * tiles - 1)
            row = tile // row_tiles
            side = (row + core) % CORES
            place[local, m] = side * chips + row // CORES * row_len + tile % row_tiles * sources
        full = table[at, row_tiles, w] > MAXK - 1
        n_full, n_less = filled

        @pl.when(full)
        def _():
            order[0, n_full] = local

        @pl.when(jnp.logical_not(full))
        def _():
            order[1, n_less] = local

        step = full.astype(jnp.int32)
        return n_full + step, n_less + 1 - step

    filled = lax.fori_loop(0, tiles, sort, (jnp.int32(0), jnp.int32(0)))

    def listed(local, m, part):
        block = kv[pl.ds(place[local, m], sources), pl.ds(part * tokens, tokens), :]
        return block.reshape(tile_len, HEAD_DIM)

    def query_of(local):
        block = own[pl.ds(local * sources, sources), pl.ds(2 * tokens, tokens), :]
        return block.reshape(tile_len, HEAD_DIM)

    def score(local, m, query, peak):
        block = lax.dot_general(
            query, listed(local, m, 0), (((1,), (1,)), ((), ())), preferred_element_type=jnp.float32
        )
        scores[m] = block
        for at in range(0, tile_len, HEAD_DIM):
            part = block[:, at : at + HEAD_DIM]
            peak = part if peak is None else jnp.maximum(peak, part)
        return peak

    def weigh(local, m, peak, total):
        probs = jnp.exp2((scores[m] - peak) * factor).astype(jnp.bfloat16)
        value = listed(local, m, 1)
        value = jnp.concatenate([value, jnp.ones_like(value)], axis=1)
        return total + jnp.dot(probs, value, preferred_element_type=jnp.float32)

    def finish(local):
        out = totals[:, :HEAD_DIM] / totals[:, HEAD_DIM:]
        outs[pl.ds(local * sources, sources)] = out.astype(outs.dtype).reshape(
            sources, tokens, HEAD_DIM
        )

    def pair(before, this, then, count):
        query = query_of(then)
        finish(before)
        peak = jnp.max(peaks[...], axis=-1, keepdims=True)
        peak = jnp.broadcast_to(peak, (tile_len, tile_len))
        total = jnp.zeros((tile_len, 2 * HEAD_DIM), jnp.float32)
        then_peak = None
        for m in range(count):
            total = weigh(this, m, peak, total)
            then_peak = score(then, m, query, then_peak)
        peaks[...] = then_peak
        totals[...] = total

    for kind, count in enumerate((MAXK, MAXK - 1)):
        number = filled[kind]

        def pick(i, kind=kind, number=number):
            return order[kind, jnp.minimum(i, number - 1)]

        def first(count=count, pick=pick):
            local = pick(0)
            query, peak = query_of(local), None
            for m in range(count):
                peak = score(local, m, query, peak)
            peaks[...] = peak

        pl.when(number > 0)(first)

        def step(i, carry, count=count, pick=pick):
            pair(pick(jnp.maximum(i - 1, 0)), pick(i), pick(i + 1), count)
            return carry

        lax.fori_loop(0, number, step, 0)
        pl.when(number > 0)(lambda pick=pick, number=number: finish(pick(number - 1)))


def attend_call(own, sib, *, row_len, row_tiles):
    chips, tokens = own.shape[0], sib.shape[1] // 2
    sources = row_len // row_tiles
    tiles = chips // sources
    tile_len = sources * tokens
    flops = 4 * tiles * tile_len * MAXK * tile_len * HEAD_DIM
    vmem = pl.BlockSpec(memory_space=pltpu.VMEM)
    return pl.pallas_call(
        functools.partial(attend_kernel, row_len=row_len, row_tiles=row_tiles),
        in_specs=[vmem, vmem],
        out_specs=vmem,
        scratch_shapes=[
            pltpu.VMEM((CORES * chips, 2 * tokens, HEAD_DIM), jnp.bfloat16),
            pltpu.VMEM((MAXK, tile_len, tile_len), jnp.float32),
            pltpu.VMEM((tile_len, HEAD_DIM), jnp.float32),
            pltpu.VMEM((tile_len, 2 * HEAD_DIM), jnp.float32),
            pltpu.VMEM((chips // row_len, 8, HEAD_DIM), jnp.int32),
            pltpu.SMEM((chips // row_len, 8, HEAD_DIM), jnp.int32),
            pltpu.SMEM((tiles, MAXK), jnp.int32),
            pltpu.SMEM((2, tiles), jnp.int32),
            pltpu.SemaphoreType.DMA((1,)),
        ],
        out_shape=jax.ShapeDtypeStruct((chips, tokens, HEAD_DIM), jnp.bfloat16),
        compiler_params=pltpu.CompilerParams(vmem_limit_bytes=24 * MIB),
        cost_estimate=pl.CostEstimate(
            flops=flops, bytes_accessed=12 * MIB, transcendentals=flops // (4 * HEAD_DIM)
        ),
        name="attend",
    )(own, sib)


def local(queries, keys, values, pairs, pair_count):
    axes = ("seq", "head")
    rows_all = lax.axis_size("seq")
    head_size = lax.axis_size("head")
    tokens, width = queries.shape
    heads = width // HEAD_DIM
    row_tiles = pairs.shape[0]
    chips = rows_all * head_size // CORES
    slot = 3 * tokens + TABLE_ROWS
    same_core = [
        [s * head_size + h for s in range(core, rows_all, CORES) for h in range(head_size)]
        for core in range(CORES)
    ]

    some = heads // PACK_STEPS
    packed = pl.pallas_call(
        pack_kernel,
        grid=(PACK_STEPS,),
        in_specs=[pl.BlockSpec((tokens, some * HEAD_DIM), lambda i: (0, i))] * 3
        + [
            pl.BlockSpec((row_tiles, MAXK), lambda i: (0, 0)),
            pl.BlockSpec((1, row_tiles), lambda i: (0, 0)),
        ],
        out_specs=pl.BlockSpec((some, slot, HEAD_DIM), lambda i: (i, 0, 0)),
        out_shape=jax.ShapeDtypeStruct((chips, slot, HEAD_DIM), jnp.bfloat16),
        scratch_shapes=[pltpu.VMEM((TABLE_ROWS, HEAD_DIM), jnp.float32)],
        compiler_params=pltpu.CompilerParams(vmem_limit_bytes=56 * MIB),
        name="pack",
    )(queries, keys, values, pairs, pair_count.reshape(1, row_tiles))
    own = lax.all_to_all(
        packed, axes, split_axis=0, concat_axis=0, tiled=True, axis_index_groups=same_core
    )
    swap = [(s, s ^ 1) for s in range(rows_all)]
    sib = lax.ppermute(own[:, : 2 * tokens], "seq", swap)
    attended = attend_call(own, sib, row_len=head_size, row_tiles=row_tiles)
    back = lax.all_to_all(
        attended, axes, split_axis=0, concat_axis=0, tiled=True, axis_index_groups=same_core
    )
    return back[:heads].transpose(1, 0, 2).reshape(tokens, width)


def solution(mesh):
    placed = (
        P(("seq", "head"), None),
        P(("seq", "head"), None),
        P(("seq", "head"), None),
        P("seq", None),
        P("seq"),
    )
    return jax.shard_map(
        local, mesh=mesh, in_specs=placed, out_specs=P(("seq", "head"), None), check_vma=False
    )
```

```python
import functools
import math

import jax
import jax.numpy as jnp
from jax import lax
from jax.experimental import pallas as pl
from jax.experimental.pallas import tpu as pltpu
from jax.sharding import PartitionSpec as P

HEAD_DIM = 128
MAXK = 4
CORES = 2
TABLE_ROWS = 16
PACK_STEPS = 2
SELF_UNROLL = 2
MIB = 1 << 20


def pack_kernel(q_ref, k_ref, v_ref, pairs_ref, count_ref, o_ref, table):
    tokens, width = q_ref.shape
    row_tiles = pairs_ref.shape[0]
    table[...] = jnp.zeros_like(table)
    table[pl.ds(0, row_tiles), pl.ds(0, MAXK)] = pairs_ref[...].astype(jnp.float32)
    table[pl.ds(row_tiles, 1), pl.ds(0, row_tiles)] = count_ref[...].astype(jnp.float32)
    for h in range(width // HEAD_DIM):
        cols = pl.ds(h * HEAD_DIM, HEAD_DIM)
        for part, ref in enumerate((k_ref, v_ref, q_ref)):
            o_ref[h, pl.ds(part * tokens, tokens), :] = ref[:, cols]
        o_ref[h, pl.ds(3 * tokens, TABLE_ROWS), :] = table[...].astype(jnp.bfloat16)


def rows_of(ref, first, sources, part, tokens):
    block = ref[pl.ds(first, sources), pl.ds(part * tokens, tokens), :]
    return block.reshape(sources * tokens, HEAD_DIM)


def product(query, key):
    return lax.dot_general(
        query, key, (((1,), (1,)), ((), ())), preferred_element_type=jnp.float32
    )


def with_ones(value):
    return jnp.concatenate([value, jnp.ones_like(value)], axis=1)


def self_kernel(own, totals, peaks, *, sources, tokens):
    tile_len = sources * tokens
    factor = math.log2(math.e) / math.sqrt(HEAD_DIM)

    def step(i, carry):
        tiles = [i * SELF_UNROLL + u for u in range(SELF_UNROLL)]
        key, value, query = (
            [rows_of(own, tile * sources, sources, part, tokens) for tile in tiles]
            for part in range(3)
        )
        scores = [product(q, k) for q, k in zip(query, key)]
        for tile, block, v in zip(tiles, scores, value):
            peak = jnp.max(block, axis=-1, keepdims=True)
            probs = jnp.exp2((block - peak) * factor).astype(jnp.bfloat16)
            totals[tile] = jnp.dot(probs, with_ones(v), preferred_element_type=jnp.float32)
            peaks[tile] = jnp.broadcast_to(peak, (tile_len, HEAD_DIM))
        return carry

    lax.fori_loop(0, peaks.shape[0] // SELF_UNROLL, step, 0)


def attend_kernel(own, sib, base_totals, base_peaks, outs, *scratch, row_len, row_tiles):
    kv, scores, peaks, totals, rows_int, table, place, order, table_sem = scratch
    chips, tokens, _ = outs.shape
    sources = row_len // row_tiles
    tile_len = sources * tokens
    tiles = chips // sources
    core = lax.axis_index("seq") % CORES
    factor = math.log2(math.e) / math.sqrt(HEAD_DIM)

    for row in range(chips // row_len):
        block = own[row * row_len, pl.ds(3 * tokens, TABLE_ROWS), :].astype(jnp.float32)
        rows_int[row] = block[: rows_int.shape[1]].astype(jnp.int32)
    spread = pltpu.make_async_copy(rows_int, table, table_sem.at[0])
    spread.start()

    def gather(source, carry):
        kv[source] = own[source, pl.ds(0, 2 * tokens), :]
        kv[chips + source] = sib[source]
        return carry

    lax.fori_loop(0, chips, gather, 0)
    spread.wait()

    def sort(local, filled):
        at, w = local // row_tiles, local % row_tiles
        for m in range(MAXK):
            tile = jnp.clip(table[at, w, m], 0, CORES * tiles - 1)
            row = tile // row_tiles
            side = (row + core) % CORES
            place[local, m] = side * chips + row // CORES * row_len + tile % row_tiles * sources
        full = table[at, row_tiles, w] > MAXK - 1
        n_full, n_less = filled

        @pl.when(full)
        def _():
            order[0, n_full] = local

        @pl.when(jnp.logical_not(full))
        def _():
            order[1, n_less] = local

        step = full.astype(jnp.int32)
        return n_full + step, n_less + 1 - step

    filled = lax.fori_loop(0, tiles, sort, (jnp.int32(0), jnp.int32(0)))

    def listed(local, m, part):
        return rows_of(kv, place[local, m], sources, part, tokens)

    def query_of(local):
        return rows_of(own, local * sources, sources, 2, tokens)

    def score(local, m, query, peak):
        block = product(query, listed(local, m, 0))
        scores[m - 1] = block
        for at in range(0, tile_len, HEAD_DIM):
            peak = jnp.maximum(peak, block[:, at : at + HEAD_DIM])
        return peak

    def weigh(local, m, peak, total):
        probs = jnp.exp2((scores[m - 1] - peak) * factor).astype(jnp.bfloat16)
        value = with_ones(listed(local, m, 1))
        return total + jnp.dot(probs, value, preferred_element_type=jnp.float32)

    def finish(local):
        out = totals[:, :HEAD_DIM] / totals[:, HEAD_DIM:]
        outs[pl.ds(local * sources, sources)] = out.astype(outs.dtype).reshape(
            sources, tokens, HEAD_DIM
        )

    def pair(before, this, then, count):
        query = query_of(then)
        finish(before)
        peak = jnp.max(peaks[...], axis=-1, keepdims=True)
        scale = jnp.exp2((base_peaks[this] - peak) * factor)
        total = base_totals[this] * jnp.concatenate([scale, scale], axis=1)
        peak = jnp.broadcast_to(peak, (tile_len, tile_len))
        then_peak = base_peaks[then]
        for m in range(1, count):
            total = weigh(this, m, peak, total)
            then_peak = score(then, m, query, then_peak)
        peaks[...] = then_peak
        totals[...] = total

    for kind, count in enumerate((MAXK, MAXK - 1)):
        number = filled[kind]

        def pick(i, kind=kind, number=number):
            return order[kind, jnp.minimum(i, number - 1)]

        def first(count=count, pick=pick):
            local = pick(0)
            query, peak = query_of(local), base_peaks[local]
            for m in range(1, count):
                peak = score(local, m, query, peak)
            peaks[...] = peak

        pl.when(number > 0)(first)

        def step(i, carry, count=count, pick=pick):
            pair(pick(jnp.maximum(i - 1, 0)), pick(i), pick(i + 1), count)
            return carry

        lax.fori_loop(0, number, step, 0)
        pl.when(number > 0)(lambda pick=pick, number=number: finish(pick(number - 1)))


def self_call(own, *, tokens, sources):
    tiles, tile_len = own.shape[0] // sources, sources * tokens
    flops = 4 * tiles * tile_len * tile_len * HEAD_DIM
    vmem = pl.BlockSpec(memory_space=pltpu.VMEM)
    return pl.pallas_call(
        functools.partial(self_kernel, sources=sources, tokens=tokens),
        in_specs=[vmem],
        out_specs=[vmem, vmem],
        out_shape=[
            jax.ShapeDtypeStruct((tiles, tile_len, 2 * HEAD_DIM), jnp.float32),
            jax.ShapeDtypeStruct((tiles, tile_len, HEAD_DIM), jnp.float32),
        ],
        compiler_params=pltpu.CompilerParams(vmem_limit_bytes=24 * MIB),
        cost_estimate=pl.CostEstimate(
            flops=flops, bytes_accessed=12 * MIB, transcendentals=flops // (4 * HEAD_DIM)
        ),
        name="attend_self",
    )(own)


def attend_call(own, sib, totals, peaks, *, row_len, row_tiles):
    chips, tokens = own.shape[0], sib.shape[1] // 2
    sources = row_len // row_tiles
    tiles, tile_len, _ = peaks.shape
    flops = 4 * tiles * tile_len * (MAXK - 1) * tile_len * HEAD_DIM
    vmem = pl.BlockSpec(memory_space=pltpu.VMEM)
    return pl.pallas_call(
        functools.partial(attend_kernel, row_len=row_len, row_tiles=row_tiles),
        in_specs=[vmem] * 4,
        out_specs=vmem,
        scratch_shapes=[
            pltpu.VMEM((CORES * chips, 2 * tokens, HEAD_DIM), jnp.bfloat16),
            pltpu.VMEM((MAXK - 1, tile_len, tile_len), jnp.float32),
            pltpu.VMEM((tile_len, HEAD_DIM), jnp.float32),
            pltpu.VMEM((tile_len, 2 * HEAD_DIM), jnp.float32),
            pltpu.VMEM((chips // row_len, 8, HEAD_DIM), jnp.int32),
            pltpu.SMEM((chips // row_len, 8, HEAD_DIM), jnp.int32),
            pltpu.SMEM((tiles, MAXK), jnp.int32),
            pltpu.SMEM((2, tiles), jnp.int32),
            pltpu.SemaphoreType.DMA((1,)),
        ],
        out_shape=jax.ShapeDtypeStruct((chips, tokens, HEAD_DIM), jnp.bfloat16),
        compiler_params=pltpu.CompilerParams(vmem_limit_bytes=24 * MIB),
        cost_estimate=pl.CostEstimate(
            flops=flops, bytes_accessed=12 * MIB, transcendentals=flops // (4 * HEAD_DIM)
        ),
        name="attend",
    )(own, sib, totals, peaks)


def local(queries, keys, values, pairs, pair_count):
    axes = ("seq", "head")
    rows_all = lax.axis_size("seq")
    head_size = lax.axis_size("head")
    tokens, width = queries.shape
    heads = width // HEAD_DIM
    row_tiles = pairs.shape[0]
    chips = rows_all * head_size // CORES
    slot = 3 * tokens + TABLE_ROWS
    same_core = [
        [s * head_size + h for s in range(core, rows_all, CORES) for h in range(head_size)]
        for core in range(CORES)
    ]

    some = heads // PACK_STEPS
    packed = pl.pallas_call(
        pack_kernel,
        grid=(PACK_STEPS,),
        in_specs=[pl.BlockSpec((tokens, some * HEAD_DIM), lambda i: (0, i))] * 3
        + [
            pl.BlockSpec((row_tiles, MAXK), lambda i: (0, 0)),
            pl.BlockSpec((1, row_tiles), lambda i: (0, 0)),
        ],
        out_specs=pl.BlockSpec((some, slot, HEAD_DIM), lambda i: (i, 0, 0)),
        out_shape=jax.ShapeDtypeStruct((chips, slot, HEAD_DIM), jnp.bfloat16),
        scratch_shapes=[pltpu.VMEM((TABLE_ROWS, HEAD_DIM), jnp.float32)],
        compiler_params=pltpu.CompilerParams(vmem_limit_bytes=56 * MIB),
        name="pack",
    )(queries, keys, values, pairs, pair_count.reshape(1, row_tiles))
    own = lax.all_to_all(
        packed, axes, split_axis=0, concat_axis=0, tiled=True, axis_index_groups=same_core
    )
    swap = [(s, s ^ 1) for s in range(rows_all)]
    sib = lax.ppermute(own[:, : 2 * tokens], "seq", swap)
    totals, peaks = self_call(own, tokens=tokens, sources=head_size // row_tiles)
    attended = attend_call(own, sib, totals, peaks, row_len=head_size, row_tiles=row_tiles)
    back = lax.all_to_all(
        attended, axes, split_axis=0, concat_axis=0, tiled=True, axis_index_groups=same_core
    )
    return back[:heads].transpose(1, 0, 2).reshape(tokens, width)


def solution(mesh):
    placed = (
        P(("seq", "head"), None),
        P(("seq", "head"), None),
        P(("seq", "head"), None),
        P("seq", None),
        P("seq"),
    )
    return jax.shard_map(
        local, mesh=mesh, in_specs=placed, out_specs=P(("seq", "head"), None), check_vma=False
    )
```

```python
import functools
import math

import jax
import jax.numpy as jnp
from jax import lax
from jax.experimental import pallas as pl
from jax.experimental.pallas import tpu as pltpu
from jax.sharding import PartitionSpec as P

HEAD_DIM = 128
MAXK = 4
CORES = 2
TABLE_ROWS = 16
PACK_STEPS = 2
SELF_UNROLL = 4
ORDER, FILLED = MAXK, MAXK + 2
MIB = 1 << 20


def pack_kernel(q_ref, k_ref, v_ref, pairs_ref, count_ref, o_ref, table):
    tokens, width = q_ref.shape
    row_tiles = pairs_ref.shape[0]
    table[...] = jnp.zeros_like(table)
    table[pl.ds(0, row_tiles), pl.ds(0, MAXK)] = pairs_ref[...].astype(jnp.float32)
    table[pl.ds(row_tiles, 1), pl.ds(0, row_tiles)] = count_ref[...].astype(jnp.float32)
    for h in range(width // HEAD_DIM):
        cols = pl.ds(h * HEAD_DIM, HEAD_DIM)
        for part, ref in enumerate((k_ref, v_ref, q_ref)):
            o_ref[h, pl.ds(part * tokens, tokens), :] = ref[:, cols]
        o_ref[h, pl.ds(3 * tokens, TABLE_ROWS), :] = table[...].astype(jnp.bfloat16)


def rows_of(ref, first, sources, part, tokens):
    block = ref[pl.ds(first, sources), pl.ds(part * tokens, tokens), :]
    return block.reshape(sources * tokens, HEAD_DIM)


def product(query, key):
    return lax.dot_general(
        query, key, (((1,), (1,)), ((), ())), preferred_element_type=jnp.float32
    )


def with_ones(value):
    return jnp.concatenate([value, jnp.ones_like(value)], axis=1)


def self_kernel(own, totals, peaks, info, rows_int, table, table_sem, *, row_len, row_tiles):
    chips, tokens = own.shape[0], (own.shape[1] - TABLE_ROWS) // 3
    sources = row_len // row_tiles
    tile_len = sources * tokens
    tiles = chips // sources
    core = lax.axis_index("seq") % CORES
    factor = math.log2(math.e) / math.sqrt(HEAD_DIM)

    for row in range(chips // row_len):
        block = own[row * row_len, pl.ds(3 * tokens, TABLE_ROWS), :].astype(jnp.float32)
        rows_int[row] = block[: rows_int.shape[1]].astype(jnp.int32)
    spread = pltpu.make_async_copy(rows_int, table, table_sem.at[0])
    spread.start()

    def step(i, carry):
        some = [i * SELF_UNROLL + u for u in range(SELF_UNROLL)]
        key, value, query = (
            [rows_of(own, tile * sources, sources, part, tokens) for tile in some]
            for part in range(3)
        )
        scores = [product(q, k) for q, k in zip(query, key)]
        for tile, block, v in zip(some, scores, value):
            peak = jnp.max(block, axis=-1, keepdims=True)
            probs = jnp.exp2((block - peak) * factor).astype(jnp.bfloat16)
            totals[tile] = jnp.dot(probs, with_ones(v), preferred_element_type=jnp.float32)
            peaks[tile] = jnp.broadcast_to(peak, (tile_len, HEAD_DIM))
        return carry

    lax.fori_loop(0, tiles // SELF_UNROLL, step, 0)
    spread.wait()

    def sort(local, filled):
        at, w = local // row_tiles, local % row_tiles
        for m in range(1, MAXK):
            tile = jnp.clip(table[at, w, m], 0, CORES * tiles - 1)
            row = tile // row_tiles
            side = (row + core) % CORES
            info[local, m] = side * chips + row // CORES * row_len + tile % row_tiles * sources
        full = table[at, row_tiles, w] > MAXK - 1
        n_full, n_less = filled

        @pl.when(full)
        def _():
            info[n_full, ORDER] = local

        @pl.when(jnp.logical_not(full))
        def _():
            info[n_less, ORDER + 1] = local

        step = full.astype(jnp.int32)
        return n_full + step, n_less + 1 - step

    n_full, n_less = lax.fori_loop(0, tiles, sort, (jnp.int32(0), jnp.int32(0)))
    info[0, FILLED] = n_full
    info[0, FILLED + 1] = n_less


def attend_kernel(own, sib, base_totals, base_peaks, info, outs, scores, peaks, totals, *, sources):
    chips, tokens, _ = outs.shape
    tile_len = sources * tokens
    factor = math.log2(math.e) / math.sqrt(HEAD_DIM)

    def listed(local, m, part):
        place = info[local, m]
        beside = place >= chips
        first = jnp.where(beside, place - chips, place)
        here = rows_of(own, first, sources, part, tokens)
        there = rows_of(sib, first, sources, part, tokens)
        return jnp.where(beside, there, here)

    def query_of(local):
        return rows_of(own, local * sources, sources, 2, tokens)

    def score(local, m, query, peak):
        block = product(query, listed(local, m, 0))
        scores[m - 1] = block
        for at in range(0, tile_len, HEAD_DIM):
            peak = jnp.maximum(peak, block[:, at : at + HEAD_DIM])
        return peak

    def weigh(local, m, peak, total):
        probs = jnp.exp2((scores[m - 1] - peak) * factor).astype(jnp.bfloat16)
        value = with_ones(listed(local, m, 1))
        return total + jnp.dot(probs, value, preferred_element_type=jnp.float32)

    def finish(local):
        out = totals[:, :HEAD_DIM] / totals[:, HEAD_DIM:]
        outs[pl.ds(local * sources, sources)] = out.astype(outs.dtype).reshape(
            sources, tokens, HEAD_DIM
        )

    def pair(before, this, then, count):
        query = query_of(then)
        finish(before)
        peak = jnp.max(peaks[...], axis=-1, keepdims=True)
        scale = jnp.exp2((base_peaks[this] - peak) * factor)
        total = base_totals[this] * jnp.concatenate([scale, scale], axis=1)
        peak = jnp.broadcast_to(peak, (tile_len, tile_len))
        then_peak = base_peaks[then]
        for m in range(1, count):
            total = weigh(this, m, peak, total)
            then_peak = score(then, m, query, then_peak)
        peaks[...] = then_peak
        totals[...] = total

    for kind, count in enumerate((MAXK, MAXK - 1)):
        number = info[0, FILLED + kind]

        def pick(i, kind=kind, number=number):
            return info[jnp.minimum(i, number - 1), ORDER + kind]

        def first(count=count, pick=pick):
            local = pick(0)
            query, peak = query_of(local), base_peaks[local]
            for m in range(1, count):
                peak = score(local, m, query, peak)
            peaks[...] = peak

        pl.when(number > 0)(first)

        def step(i, carry, count=count, pick=pick):
            pair(pick(jnp.maximum(i - 1, 0)), pick(i), pick(i + 1), count)
            return carry

        lax.fori_loop(0, number, step, 0)
        pl.when(number > 0)(lambda pick=pick, number=number: finish(pick(number - 1)))


def self_call(own, *, row_len, row_tiles):
    chips, tokens = own.shape[0], (own.shape[1] - TABLE_ROWS) // 3
    sources = row_len // row_tiles
    tiles, tile_len = chips // sources, sources * tokens
    flops = 4 * tiles * tile_len * tile_len * HEAD_DIM
    vmem = pl.BlockSpec(memory_space=pltpu.VMEM)
    return pl.pallas_call(
        functools.partial(self_kernel, row_len=row_len, row_tiles=row_tiles),
        in_specs=[vmem],
        out_specs=[vmem, vmem, pl.BlockSpec(memory_space=pltpu.SMEM)],
        scratch_shapes=[
            pltpu.VMEM((chips // row_len, 8, HEAD_DIM), jnp.int32),
            pltpu.SMEM((chips // row_len, 8, HEAD_DIM), jnp.int32),
            pltpu.SemaphoreType.DMA((1,)),
        ],
        out_shape=[
            jax.ShapeDtypeStruct((tiles, tile_len, 2 * HEAD_DIM), jnp.float32),
            jax.ShapeDtypeStruct((tiles, tile_len, HEAD_DIM), jnp.float32),
            jax.ShapeDtypeStruct((tiles, FILLED + 2), jnp.int32),
        ],
        compiler_params=pltpu.CompilerParams(vmem_limit_bytes=24 * MIB),
        cost_estimate=pl.CostEstimate(
            flops=flops, bytes_accessed=12 * MIB, transcendentals=flops // (4 * HEAD_DIM)
        ),
        name="attend_self",
    )(own)


def attend_call(own, sib, totals, peaks, info, *, sources):
    chips, tokens = own.shape[0], sib.shape[1] // 2
    tiles, tile_len, _ = peaks.shape
    flops = 4 * tiles * tile_len * (MAXK - 1) * tile_len * HEAD_DIM
    vmem = pl.BlockSpec(memory_space=pltpu.VMEM)
    return pl.pallas_call(
        functools.partial(attend_kernel, sources=sources),
        in_specs=[vmem] * 4 + [pl.BlockSpec(memory_space=pltpu.SMEM)],
        out_specs=vmem,
        scratch_shapes=[
            pltpu.VMEM((MAXK - 1, tile_len, tile_len), jnp.float32),
            pltpu.VMEM((tile_len, HEAD_DIM), jnp.float32),
            pltpu.VMEM((tile_len, 2 * HEAD_DIM), jnp.float32),
        ],
        out_shape=jax.ShapeDtypeStruct((chips, tokens, HEAD_DIM), jnp.bfloat16),
        compiler_params=pltpu.CompilerParams(vmem_limit_bytes=24 * MIB),
        cost_estimate=pl.CostEstimate(
            flops=flops, bytes_accessed=12 * MIB, transcendentals=flops // (4 * HEAD_DIM)
        ),
        name="attend",
    )(own, sib, totals, peaks, info)


def local(queries, keys, values, pairs, pair_count):
    axes = ("seq", "head")
    rows_all = lax.axis_size("seq")
    head_size = lax.axis_size("head")
    tokens, width = queries.shape
    heads = width // HEAD_DIM
    row_tiles = pairs.shape[0]
    chips = rows_all * head_size // CORES
    slot = 3 * tokens + TABLE_ROWS
    same_core = [
        [s * head_size + h for s in range(core, rows_all, CORES) for h in range(head_size)]
        for core in range(CORES)
    ]

    some = heads // PACK_STEPS
    packed = pl.pallas_call(
        pack_kernel,
        grid=(PACK_STEPS,),
        in_specs=[pl.BlockSpec((tokens, some * HEAD_DIM), lambda i: (0, i))] * 3
        + [
            pl.BlockSpec((row_tiles, MAXK), lambda i: (0, 0)),
            pl.BlockSpec((1, row_tiles), lambda i: (0, 0)),
        ],
        out_specs=pl.BlockSpec((some, slot, HEAD_DIM), lambda i: (i, 0, 0)),
        out_shape=jax.ShapeDtypeStruct((chips, slot, HEAD_DIM), jnp.bfloat16),
        scratch_shapes=[pltpu.VMEM((TABLE_ROWS, HEAD_DIM), jnp.float32)],
        compiler_params=pltpu.CompilerParams(vmem_limit_bytes=56 * MIB),
        name="pack",
    )(queries, keys, values, pairs, pair_count.reshape(1, row_tiles))
    own = lax.all_to_all(
        packed, axes, split_axis=0, concat_axis=0, tiled=True, axis_index_groups=same_core
    )
    swap = [(s, s ^ 1) for s in range(rows_all)]
    sib = lax.ppermute(own[:, : 2 * tokens], "seq", swap)
    totals, peaks, info = self_call(own, row_len=head_size, row_tiles=row_tiles)
    attended = attend_call(own, sib, totals, peaks, info, sources=head_size // row_tiles)
    back = lax.all_to_all(
        attended, axes, split_axis=0, concat_axis=0, tiled=True, axis_index_groups=same_core
    )
    return back[:heads].transpose(1, 0, 2).reshape(tokens, width)


def solution(mesh):
    placed = (
        P(("seq", "head"), None),
        P(("seq", "head"), None),
        P(("seq", "head"), None),
        P("seq", None),
        P("seq"),
    )
    return jax.shard_map(
        local, mesh=mesh, in_specs=placed, out_specs=P(("seq", "head"), None), check_vma=False
    )
```

```python
import functools
import math

import jax
import jax.numpy as jnp
from jax import lax
from jax.experimental import pallas as pl
from jax.experimental.pallas import tpu as pltpu
from jax.sharding import PartitionSpec as P

HEAD_DIM = 128
MAXK = 4
CORES = 2
TABLE_ROWS = 16
PACK_STEPS = 2
SELF_UNROLL = 4
ORDER, FILLED = MAXK, MAXK + 2
MIB = 1 << 20


def pack_kernel(q_ref, k_ref, v_ref, pairs_ref, count_ref, o_ref, table):
    tokens, width = q_ref.shape
    row_tiles = pairs_ref.shape[0]
    table[...] = jnp.zeros_like(table)
    table[pl.ds(0, row_tiles), pl.ds(0, MAXK)] = pairs_ref[...].astype(jnp.float32)
    table[pl.ds(row_tiles, 1), pl.ds(0, row_tiles)] = count_ref[...].astype(jnp.float32)
    for h in range(width // HEAD_DIM):
        cols = pl.ds(h * HEAD_DIM, HEAD_DIM)
        for part, ref in enumerate((k_ref, v_ref, q_ref)):
            o_ref[h, pl.ds(part * tokens, tokens), :] = ref[:, cols]
        o_ref[h, pl.ds(3 * tokens, TABLE_ROWS), :] = table[...].astype(jnp.bfloat16)


def rows_of(ref, first, sources, part, tokens):
    block = ref[pl.ds(first, sources), pl.ds(part * tokens, tokens), :]
    return block.reshape(sources * tokens, HEAD_DIM)


def product(query, key):
    return lax.dot_general(
        query, key, (((1,), (1,)), ((), ())), preferred_element_type=jnp.float32
    )


def with_ones(value):
    return jnp.concatenate([value, jnp.ones_like(value)], axis=1)


def self_kernel(own, totals, peaks, info, rows_int, table, table_sem, *, row_len, row_tiles):
    chips, tokens = own.shape[0], (own.shape[1] - TABLE_ROWS) // 3
    sources = row_len // row_tiles
    tile_len = sources * tokens
    tiles = chips // sources
    core = lax.axis_index("seq") % CORES
    factor = math.log2(math.e) / math.sqrt(HEAD_DIM)

    for row in range(chips // row_len):
        block = own[row * row_len, pl.ds(3 * tokens, TABLE_ROWS), :].astype(jnp.float32)
        rows_int[row] = block[: rows_int.shape[1]].astype(jnp.int32)
    spread = pltpu.make_async_copy(rows_int, table, table_sem.at[0])
    spread.start()

    def step(i, carry):
        some = [i * SELF_UNROLL + u for u in range(SELF_UNROLL)]
        key, value, query = (
            [rows_of(own, tile * sources, sources, part, tokens) for tile in some]
            for part in range(3)
        )
        scores = [product(q, k) for q, k in zip(query, key)]
        for tile, block, v in zip(some, scores, value):
            peak = jnp.max(block, axis=-1, keepdims=True)
            probs = jnp.exp2((block - peak) * factor).astype(jnp.bfloat16)
            totals[tile] = jnp.dot(probs, with_ones(v), preferred_element_type=jnp.float32)
            peaks[tile] = jnp.broadcast_to(peak, (tile_len, HEAD_DIM))
        return carry

    lax.fori_loop(0, tiles // SELF_UNROLL, step, 0)
    spread.wait()

    def sort(local, filled):
        at, w = local // row_tiles, local % row_tiles
        for m in range(1, MAXK):
            tile = jnp.clip(table[at, w, m], 0, CORES * tiles - 1)
            row = tile // row_tiles
            side = (row + core) % CORES
            info[local, m] = side * chips + row // CORES * row_len + tile % row_tiles * sources
        full = table[at, row_tiles, w] > MAXK - 1
        n_full, n_less = filled

        info[n_full, ORDER] = local
        info[n_less, ORDER + 1] = local
        step = full.astype(jnp.int32)
        return n_full + step, n_less + 1 - step

    n_full, n_less = lax.fori_loop(0, tiles, sort, (jnp.int32(0), jnp.int32(0)))
    info[0, FILLED] = n_full
    info[0, FILLED + 1] = n_less


def attend_kernel(own, sib, base_totals, base_peaks, info, outs, scores, peaks, totals, *, sources):
    chips, tokens, _ = outs.shape
    tile_len = sources * tokens
    factor = math.log2(math.e) / math.sqrt(HEAD_DIM)

    def listed(local, m, part):
        place = info[local, m]
        beside = place >= chips
        first = jnp.where(beside, place - chips, place)
        here = rows_of(own, first, sources, part, tokens)
        there = rows_of(sib, first, sources, part, tokens)
        return jnp.where(beside, there, here)

    def query_of(local):
        return rows_of(own, local * sources, sources, 2, tokens)

    def score(local, m, query, peak):
        block = product(query, listed(local, m, 0))
        scores[m - 1] = block
        for at in range(0, tile_len, HEAD_DIM):
            peak = jnp.maximum(peak, block[:, at : at + HEAD_DIM])
        return peak

    def weigh(local, m, peak, total):
        probs = jnp.exp2((scores[m - 1] - peak) * factor).astype(jnp.bfloat16)
        value = with_ones(listed(local, m, 1))
        return total + jnp.dot(probs, value, preferred_element_type=jnp.float32)

    def finish(local):
        out = totals[:, :HEAD_DIM] / totals[:, HEAD_DIM:]
        outs[pl.ds(local * sources, sources)] = out.astype(outs.dtype).reshape(
            sources, tokens, HEAD_DIM
        )

    def pair(before, this, then, count):
        query = query_of(then)
        finish(before)
        peak = jnp.max(peaks[...], axis=-1, keepdims=True)
        scale = jnp.exp2((base_peaks[this] - peak) * factor)
        total = base_totals[this] * jnp.concatenate([scale, scale], axis=1)
        peak = jnp.broadcast_to(peak, (tile_len, tile_len))
        then_peak = base_peaks[then]
        for m in range(1, count):
            total = weigh(this, m, peak, total)
            then_peak = score(then, m, query, then_peak)
        peaks[...] = then_peak
        totals[...] = total

    for kind, count in enumerate((MAXK, MAXK - 1)):
        number = info[0, FILLED + kind]

        def pick(i, kind=kind, number=number):
            return info[jnp.minimum(i, number - 1), ORDER + kind]

        def first(count=count, pick=pick):
            local = pick(0)
            query, peak = query_of(local), base_peaks[local]
            for m in range(1, count):
                peak = score(local, m, query, peak)
            peaks[...] = peak

        pl.when(number > 0)(first)

        def step(i, carry, count=count, pick=pick):
            pair(pick(jnp.maximum(i - 1, 0)), pick(i), pick(i + 1), count)
            return carry

        lax.fori_loop(0, number, step, 0)
        pl.when(number > 0)(lambda pick=pick, number=number: finish(pick(number - 1)))


def self_call(own, *, row_len, row_tiles):
    chips, tokens = own.shape[0], (own.shape[1] - TABLE_ROWS) // 3
    sources = row_len // row_tiles
    tiles, tile_len = chips // sources, sources * tokens
    flops = 4 * tiles * tile_len * tile_len * HEAD_DIM
    vmem = pl.BlockSpec(memory_space=pltpu.VMEM)
    return pl.pallas_call(
        functools.partial(self_kernel, row_len=row_len, row_tiles=row_tiles),
        in_specs=[vmem],
        out_specs=[vmem, vmem, pl.BlockSpec(memory_space=pltpu.SMEM)],
        scratch_shapes=[
            pltpu.VMEM((chips // row_len, 8, HEAD_DIM), jnp.int32),
            pltpu.SMEM((chips // row_len, 8, HEAD_DIM), jnp.int32),
            pltpu.SemaphoreType.DMA((1,)),
        ],
        out_shape=[
            jax.ShapeDtypeStruct((tiles, tile_len, 2 * HEAD_DIM), jnp.float32),
            jax.ShapeDtypeStruct((tiles, tile_len, HEAD_DIM), jnp.float32),
            jax.ShapeDtypeStruct((tiles, FILLED + 2), jnp.int32),
        ],
        compiler_params=pltpu.CompilerParams(vmem_limit_bytes=24 * MIB),
        cost_estimate=pl.CostEstimate(
            flops=flops, bytes_accessed=12 * MIB, transcendentals=flops // (4 * HEAD_DIM)
        ),
        name="attend_self",
    )(own)


def attend_call(own, sib, totals, peaks, info, *, sources):
    chips, tokens = own.shape[0], sib.shape[1] // 2
    tiles, tile_len, _ = peaks.shape
    flops = 4 * tiles * tile_len * (MAXK - 1) * tile_len * HEAD_DIM
    vmem = pl.BlockSpec(memory_space=pltpu.VMEM)
    return pl.pallas_call(
        functools.partial(attend_kernel, sources=sources),
        in_specs=[vmem] * 4 + [pl.BlockSpec(memory_space=pltpu.SMEM)],
        out_specs=vmem,
        scratch_shapes=[
            pltpu.VMEM((MAXK - 1, tile_len, tile_len), jnp.float32),
            pltpu.VMEM((tile_len, HEAD_DIM), jnp.float32),
            pltpu.VMEM((tile_len, 2 * HEAD_DIM), jnp.float32),
        ],
        out_shape=jax.ShapeDtypeStruct((chips, tokens, HEAD_DIM), jnp.bfloat16),
        compiler_params=pltpu.CompilerParams(vmem_limit_bytes=24 * MIB),
        cost_estimate=pl.CostEstimate(
            flops=flops, bytes_accessed=12 * MIB, transcendentals=flops // (4 * HEAD_DIM)
        ),
        name="attend",
    )(own, sib, totals, peaks, info)


def local(queries, keys, values, pairs, pair_count):
    axes = ("seq", "head")
    rows_all = lax.axis_size("seq")
    head_size = lax.axis_size("head")
    tokens, width = queries.shape
    heads = width // HEAD_DIM
    row_tiles = pairs.shape[0]
    chips = rows_all * head_size // CORES
    slot = 3 * tokens + TABLE_ROWS
    same_core = [
        [s * head_size + h for s in range(core, rows_all, CORES) for h in range(head_size)]
        for core in range(CORES)
    ]

    some = heads // PACK_STEPS
    packed = pl.pallas_call(
        pack_kernel,
        grid=(PACK_STEPS,),
        in_specs=[pl.BlockSpec((tokens, some * HEAD_DIM), lambda i: (0, i))] * 3
        + [
            pl.BlockSpec((row_tiles, MAXK), lambda i: (0, 0)),
            pl.BlockSpec((1, row_tiles), lambda i: (0, 0)),
        ],
        out_specs=pl.BlockSpec((some, slot, HEAD_DIM), lambda i: (i, 0, 0)),
        out_shape=jax.ShapeDtypeStruct((chips, slot, HEAD_DIM), jnp.bfloat16),
        scratch_shapes=[pltpu.VMEM((TABLE_ROWS, HEAD_DIM), jnp.float32)],
        compiler_params=pltpu.CompilerParams(vmem_limit_bytes=56 * MIB),
        name="pack",
    )(queries, keys, values, pairs, pair_count.reshape(1, row_tiles))
    own = lax.all_to_all(
        packed, axes, split_axis=0, concat_axis=0, tiled=True, axis_index_groups=same_core
    )
    swap = [(s, s ^ 1) for s in range(rows_all)]
    sib = lax.ppermute(own[:, : 2 * tokens], "seq", swap)
    totals, peaks, info = self_call(own, row_len=head_size, row_tiles=row_tiles)
    attended = attend_call(own, sib, totals, peaks, info, sources=head_size // row_tiles)
    back = lax.all_to_all(
        attended, axes, split_axis=0, concat_axis=0, tiled=True, axis_index_groups=same_core
    )
    return back[:heads].transpose(1, 0, 2).reshape(tokens, width)


def solution(mesh):
    placed = (
        P(("seq", "head"), None),
        P(("seq", "head"), None),
        P(("seq", "head"), None),
        P("seq", None),
        P("seq"),
    )
    return jax.shard_map(
        local, mesh=mesh, in_specs=placed, out_specs=P(("seq", "head"), None), check_vma=False
    )
```
